32 devices in a mesh: gx: 4 (over y, core), yz: 8 (over z, x).
Axes of the slice: x: 2, y: 2, z: 4, core: 2. Of those that a mesh axis runs over, the one named last changes fastest.
Arguments:
- velocity: float32 [3, 256, 256, 128], P(None, 'gx', 'yz'), may hold values from -6 to 6
- section_sum: float32 [3, 256, 256, 128], P(None, 'gx', 'yz'), may hold values from -0.3 to 0.3
- metric_x: float32 [256], P('gx'), may hold values from 0.5 to 2
- metric_y: float32 [256], P('yz'), may hold values from 0.5 to 2
Outputs:
- velocity_next: float32 [3, 256, 256, 128], P(None, 'gx', 'yz')
- section_next: float32 [3, 256, 256, 128], P(None, 'gx', 'yz')
The draws below stay inside these ranges and needn't reach their ends.
All inputs are finite; a program needn't handle non-finite values.
Results may differ from the reference program's by a relative error of at most 0.000094.
Values sent between devices are 32-bit elements; how exact they have to be, the bound alone decides.
No kernel may reach another device: no remote copies, remote signals or barrier semaphores. Data moves between devices by JAX's collectives and lax.ppermute only.
A program may use at most 64 MiB of HBM per device.

```python
import math
import jax
import jax.numpy as jnp
from jax import lax

CX = 64
NZ = 128
NX = 256
NY = 256


def draw_velocity(key, part):
    rate_key, phase_key, level_key = jax.random.split(key, 3)
    index = jnp.arange(NX, dtype=jnp.int32)
    offset = index % CX
    distance = jnp.minimum(offset, CX - offset).astype(jnp.float32)
    envelope = 0.25 + 0.75 * jnp.exp(-(distance / 12.0) ** 2)
    parity = (1 - 2 * (index % 2)).astype(jnp.float32)
    position = index.astype(jnp.float32)
    lines = (3, 1, NY, NZ)
    rate = jax.random.uniform(rate_key, lines, jnp.float32, 0.015, 0.06)
    level = jnp.exp(jax.random.uniform(level_key, lines, jnp.float32, math.log(0.5), math.log(1.5)))
    mean_flow = 1.5
    phase = jax.random.uniform(phase_key, lines, jnp.float32, -jnp.pi, jnp.pi)
    wave = jnp.cos(rate * position[None, :, None, None] + phase)
    shape_x = (envelope * parity)[None, :, None, None]
    scales = jnp.array([3.0, 0.3, 4.0], jnp.float32).reshape(3, 1, 1, 1)
    flow = jnp.array([mean_flow, 0.0, 0.0], jnp.float32).reshape(3, 1, 1, 1)
    return (scales * level * shape_x * wave + flow).astype(jnp.float32)


def block_scale(rng, shape, shards, low, largest):
    def one(axis_at, shards_of):
        draws = jax.random.uniform(jax.random.fold_in(jax.random.fold_in(rng, 6), axis_at), (shards_of,), jnp.float32, low / len(shards), largest / len(shards))
        return jnp.repeat(jnp.exp(draws), shape[axis_at] // shards_of).reshape((-1,) + (1,) * (len(shape) - axis_at - 1))

    level = one(*shards[0])
    for cut in shards[1:]:
        level = level * one(*cut)
    return level


def centred(rng, dims, width, most, cuts=(), held_as=jnp.bfloat16):
    drawn = width * jax.random.normal(rng, dims, jnp.float32)
    if cuts:
        drawn = drawn * block_scale(rng, dims, cuts, -0.22, 0.18)
    return jnp.clip(drawn, -most, most).astype(held_as)


def setup_inputs(seed: int = 0) -> dict:
    splits = jax.random.split(jax.random.key(seed), 5)
    return {
        "velocity": draw_velocity(jax.random.fold_in(splits[4], 71), 0),
        "section_sum": centred(splits[1], (3, NX, NY, NZ), 0.05, 0.3, ((1, 4), (2, 8)), jnp.float32),
        "metric_x": jnp.clip(jnp.exp(math.log(2.0) - 1.3862944 * jax.random.uniform(splits[2], (NX,), jnp.float32) ** block_scale(splits[2], (NX,), ((0, 4),), -0.2, 0.2)), 0.5, 2.0),
        "metric_y": jnp.clip(jnp.exp(math.log(2.0) - 1.3862944 * jax.random.uniform(splits[3], (NY,), jnp.float32) ** block_scale(splits[3], (NY,), ((0, 8),), -0.2, 0.2)), 0.5, 2.0),
    }


third = 1.0 / 3.0
time_step = 0.2
rk_keep = -5.0 / 9.0
rk_add = 15.0 / 16.0

def couplings(position, length):
    interior_c = jnp.where((position == 1) | (position == length - 2), jnp.float32(0.25), jnp.float32(third))
    lower_c = jnp.where(position == 0, jnp.float32(0.0), jnp.where(position == length - 1, jnp.float32(2.0), interior_c))
    upper_c = jnp.where(position == length - 1, jnp.float32(0.0), jnp.where(position == 0, jnp.float32(2.0), interior_c))
    return (lower_c, upper_c)

def compact_source(padded, position, length, extent):

    def shifted(offset):
        return padded[:, 2 + offset:2 + offset + extent]
    interior = 7.0 / 9.0 * (shifted(1) - shifted(-1)) + 1.0 / 36.0 * (shifted(2) - shifted(-2))
    near_edge = 0.75 * (shifted(1) - shifted(-1))
    first_row = -2.5 * shifted(0) + 2.0 * shifted(1) + 0.5 * shifted(2)
    last_row = 2.5 * shifted(0) - 2.0 * shifted(-1) - 0.5 * shifted(-2)
    where_x = position.reshape(1, -1, 1, 1)
    return jnp.where(where_x == 0, first_row, jnp.where(where_x == length - 1, last_row, jnp.where((where_x == 1) | (where_x == length - 2), near_edge, interior)))

def y_derivative(padded, columns):

    def shifted(offset):
        return padded[:, :, 3 + offset:3 + offset + columns]
    return 0.75 * (shifted(1) - shifted(-1)) - 0.15 * (shifted(2) - shifted(-2)) + 1.0 / 60.0 * (shifted(3) - shifted(-3))

def reference(velocity, section_sum, metric_x, metric_y):
    length = velocity.shape[1]
    columns = velocity.shape[2]
    padded = jnp.pad(velocity, ((0, 0), (2, 2), (0, 0), (0, 0)))
    position = jnp.arange(length, dtype=jnp.int32)
    source = compact_source(padded, position, length, length)
    lower_c, upper_c = couplings(position, length)
    stacked = jnp.transpose(source, (1, 0, 2, 3)).reshape(length, -1)
    solved = lax.linalg.tridiagonal_solve(lower_c, jnp.ones((length,), jnp.float32), upper_c, stacked)
    slope_x = jnp.transpose(solved.reshape(length, 3, columns, -1), (1, 0, 2, 3)) * metric_x[None, :, None, None]
    padded_y = jnp.pad(velocity, ((0, 0), (0, 0), (3, 3), (0, 0)))
    slope_y = y_derivative(padded_y, columns) * metric_y[None, None, :, None]
    tendency = -(velocity[0:1] * slope_x + velocity[1:2] * slope_y)
    section_next = rk_keep * section_sum + time_step * tendency
    return (velocity + rk_add * section_next, section_next)
```

```python
import functools

import jax
import jax.numpy as jnp
import numpy as np
from jax import lax
from jax.experimental import pallas as pl
from jax.experimental.pallas import tpu as pltpu
from jax.sharding import PartitionSpec as P

time_step = 0.2
rk_keep = -5.0 / 9.0
rk_add = 15.0 / 16.0
source_scale = 7.0 / 9.0
y_scale = -time_step * 0.75

ANY = pl.BlockSpec(memory_space=pl.ANY)
HBM = pl.BlockSpec(memory_space=pltpu.HBM)
VMEM = pl.BlockSpec(memory_space=pltpu.VMEM)
SMEM = pl.BlockSpec(memory_space=pltpu.SMEM)


def params(mib):
    return pltpu.CompilerParams(vmem_limit_bytes=mib << 20)


def vmem(shape):
    return pltpu.VMEM(shape, jnp.float32)


def cost(flops, size):
    return pl.CostEstimate(flops=flops, bytes_accessed=size, transcendentals=0)


def swaps(count):
    first = [(i, i ^ 1) for i in range(count) if i ^ 1 < count]
    second = [(i, i + 1) for i in range(1, count - 1, 2)]
    return first, second + [(j, i) for i, j in second]


class Rows:
    def __init__(self, length, extent):
        self.extent = extent
        self.blocks = length // extent
        lower = np.full(length, 1.0 / 3.0)
        upper = np.full(length, 1.0 / 3.0)
        lower[[1, -2]] = upper[[1, -2]] = 0.25
        lower[0], upper[0], lower[-1], upper[-1] = 0.0, 2.0, 2.0, 0.0
        down = np.ones(length)
        up = np.ones(length)
        for i in range(1, length):
            down[i] = 1.0 - lower[i] * upper[i - 1] / down[i - 1]
        for i in range(length - 2, -1, -1):
            up[i] = 1.0 - upper[i] * lower[i + 1] / up[i + 1]
        self.forward = np.zeros(length)
        self.forward[1:] = lower[1:] / down[:-1]
        self.backward = np.zeros(length)
        self.backward[:-1] = upper[:-1] / down[1:]
        reverse = np.zeros(length)
        reverse[:-1] = upper[:-1] / up[1:]
        self.scale = -time_step * source_scale / down
        self.decay = np.zeros(length)
        self.weight = np.ones(length)
        for i in range(length):
            before = 1.0 if i % extent == 0 else self.decay[i - 1]
            self.decay[i] = -self.forward[i] * before
            if i % extent:
                self.weight[i] = -reverse[i - 1] * self.weight[i - 1]
        self.after = np.zeros(length)
        self.closing = np.ones(length)
        self.after[:-1] = upper[:-1] / up[1:]
        self.closing[:-1] = down[:-1] / (down[:-1] - upper[:-1] * lower[1:] / up[1:])
        taps = np.tile(np.array([-1.0 / 36, -7.0 / 9, 0.0, 7.0 / 9, 1.0 / 36]), (length, 1))
        taps[[1, -2]] = [0.0, -0.75, 0.0, 0.75, 0.0]
        taps[0] = [0.0, 0.0, -2.5, 2.0, 0.5]
        taps[-1] = [-0.5, -2.0, 2.5, 0.0, 0.0]
        self.taps = taps / source_scale

    def pick(self, values, row, me):
        values = np.asarray(values, np.float64)[row :: self.extent].astype(np.float32)
        kinds, counts = np.unique(values, return_counts=True)
        common = kinds[np.argmax(counts)]
        if len(kinds) == 1:
            return float(common)
        out = jnp.float32(common)
        for block, value in enumerate(values):
            if value != common:
                out = jnp.where(me == block, jnp.float32(value), out)
        return out


def scaled(value, coefficient):
    if isinstance(coefficient, float):
        if coefficient == 0.0:
            return None
        if coefficient == 1.0:
            return value
    return value * coefficient


def total(terms):
    terms = [t for t in terms if t is not None]
    return functools.reduce(lambda a, b: a + b, terms)


def pack_y_first(v_hbm, send, tile, sem):
    comps, extent, columns, _ = v_hbm.shape
    odd = lax.rem(lax.axis_index("yz"), 2)
    start = pl.multiple_of((1 - odd) * (columns - 8), 8)
    copy = pltpu.make_async_copy(v_hbm.at[:, :, pl.ds(start, 8), :], tile, sem)
    copy.start()
    copy.wait()
    rows = tile.reshape(comps * extent * 8, tile.shape[-1])
    for side in range(2):

        @pl.when(odd == side)
        def _():
            gather_columns(rows, send, comps, extent, 0 if side else 5)


def pack_rest(v_hbm, send, first, second, tile, sem):
    comps, extent, columns, _ = v_hbm.shape
    odd = lax.rem(lax.axis_index("yz"), 2)
    odd_x = lax.rem(lax.axis_index("gx"), 2)
    start = pl.multiple_of(odd * (columns - 8), 8)
    copy = pltpu.make_async_copy(v_hbm.at[:, :, pl.ds(start, 8), :], tile, sem.at[0])
    copy_1 = pltpu.make_async_copy(v_hbm.at[:, pl.ds((1 - odd_x) * (extent - 2), 2)], first, sem.at[1])
    copy_2 = pltpu.make_async_copy(v_hbm.at[:, pl.ds(odd_x * (extent - 2), 2)], second, sem.at[2])
    copy_1.start()
    copy_2.start()
    copy.start()
    copy_1.wait()
    copy_2.wait()
    copy.wait()
    rows = tile.reshape(comps * extent * 8, tile.shape[-1])
    for side in range(2):

        @pl.when(odd == side)
        def _():
            gather_columns(rows, send, comps, extent, 5 if side else 0)


def gather_columns(rows, send, comps, extent, base):
    for c in range(comps):
        for k in range(3):
            send[c * 3 + k] = rows[pl.ds(c * extent * 8 + base + k, extent, stride=8), :]


def y_part(v_ref, my_ref, t_ref):
    comps, extent, columns, lanes = v_ref.shape
    rows = v_ref.reshape(comps * extent * columns, lanes)
    out = t_ref.reshape(comps * extent * columns, lanes)

    @pl.loop(0, extent // 8)
    def _(block):
        def at(c, j):
            return pl.ds(c * extent * columns + block * 8 * columns + j, 8, stride=columns)

        window = [[rows[at(c, j), :] for j in range(3)] for c in range(comps)]
        window = [[None, None, None] + w for w in window]
        for j in range(columns):
            for c in range(comps):
                window[c].append(rows[at(c, j + 3), :] if j + 3 < columns else None)
            factor = window[1][3] * (my_ref[j] * y_scale)
            for c in range(comps):
                w = window[c]
                slope = None
                for k, coefficient in ((1, 1.0), (2, -0.2), (3, 1.0 / 45.0)):
                    ahead, behind = w[3 + k], w[3 - k]
                    if ahead is not None and behind is not None:
                        term = ahead - behind
                    elif ahead is not None:
                        term = ahead
                    else:
                        term, coefficient = behind, -coefficient
                    term = scaled(term, coefficient)
                    slope = term if slope is None else slope + term
                out[at(c, j), :] = factor * slope
                window[c] = w[1:]


def sweep(table, v_ref, one_ref, two_ref, g_ref, send_1, send_2):
    comps, extent = v_ref.shape[:2]
    me = lax.axis_index("gx")
    even = lax.rem(me, 2) == 0
    pick = functools.partial(table.pick, me=me)
    taps = {i: [pick(table.taps[:, k], i) for k in range(5)] for i in range(extent)}
    forward = [pick(table.forward, i) for i in range(extent)]
    weight = [pick(table.weight, i) for i in range(extent)]

    @pl.loop(0, comps)
    def _(c):
        before = [jnp.where(even, two_ref[c, k], one_ref[c, k]) for k in range(2)]
        after = [jnp.where(even, one_ref[c, k], two_ref[c, k]) for k in range(2)]
        window = before + [v_ref[c, 0], v_ref[c, 1]]
        g = None
        for i in range(extent):
            window.append(v_ref[c, i + 2] if i + 2 < extent else after[i + 2 - extent])
            tap = taps[i]
            if all(isinstance(a, float) for a in tap) and tap[2] == 0.0:
                source = scaled(window[3] - window[1], tap[3]) + scaled(window[4] - window[0], tap[4])
            else:
                source = total([scaled(f, a) for f, a in zip(window, tap)])
            g = source if i == 0 else source - g * forward[i]
            reverse = source if i == 0 else reverse + source * weight[i]
            g_ref[c, i] = g
            window = window[1:]
        send_1[c] = jnp.where(even, g, reverse)
        send_2[c] = jnp.where(even, reverse, g)


def fix_columns(halo, base, block, columns, my_ref, right, load_u1, load_sum, load_v, store):
    comps = halo.shape[0] // 3
    for j in range(3):
        near = [k if right else 2 - k for k in range(3)]
        column = columns - 1 - j if right else j
        sign = 1.0 if right else -1.0
        factor = load_u1(column) * (my_ref[column] * (y_scale * sign))
        for c in range(comps):
            terms = [
                scaled(halo[c * 3 + near[k], pl.ds(block, 8), :], a)
                for k, a in zip(range(3), (1.0, -0.2, 1.0 / 45.0)[j:])
            ]
            value = load_sum(c, column) + factor * total(terms)
            store(c, column, value, load_v(c, column) + rk_add * value)


def finish(
    table, v_ref, s_ref, g_ref, t_ref, one_ref, two_ref, halo, mx_ref, my_ref,
    v_out, s_out, v_tile, s_tile, v_buf, s_buf, before, sem,
):
    comps, extent, columns, lanes = v_ref.shape
    me = lax.axis_index("gx")
    even = lax.rem(me, 2) == 0
    odd_y = lax.rem(lax.axis_index("yz"), 2)
    pick = functools.partial(table.pick, me=me)
    last = extent - 1
    state = []
    for c in range(comps):
        before[c] = jnp.where(even, two_ref[c], one_ref[c])
        after = jnp.where(even, one_ref[c], two_ref[c])
        g = g_ref[c, last] + before[c] * pick(table.decay, last)
        state.append((g - after * pick(table.after, last)) * pick(table.closing, last))
    copies = []
    v_rows, u_rows, s_rows = (r.reshape(comps * extent * columns, lanes) for r in (v_buf, v_ref, s_buf))
    for block in range(extent - 8, -1, -8):
        for i in range(block + 7, block - 1, -1):
            factor = v_ref[0, i] * (mx_ref[i] * pick(table.scale, i))
            decay = pick(table.decay, i)
            backward = pick(table.backward, i)
            for c in range(comps):
                if i < last:
                    state[c] = (g_ref[c, i] + before[c] * decay) - state[c] * backward
                value = s_ref[c, i] * rk_keep + (t_ref[c, i] + factor * state[c])
                s_buf[c, i] = value
                v_buf[c, i] = v_ref[c, i] + rk_add * value

        def at(c, j):
            return pl.ds(c * extent * columns + block * columns + j, 8, stride=columns)

        def store(c, j, section, velocity):
            s_rows[at(c, j), :] = section
            v_rows[at(c, j), :] = velocity

        for side in range(2):

            @pl.when(odd_y == side)
            def _():
                fix_columns(
                    halo, 0, block, columns, my_ref, side == 0,
                    lambda j: u_rows[at(1, j), :],
                    lambda c, j: s_rows[at(c, j), :],
                    lambda c, j: u_rows[at(c, j), :],
                    store,
                )

        keep = pl.multiple_of((1 - odd_y) * 8, 8)
        rest = pl.multiple_of(odd_y * (columns - 8), 8)
        for n, (buf, out, tile) in enumerate(((v_buf, v_out, v_tile), (s_buf, s_out, s_tile))):
            here = pl.ds(block, 8)
            copy = pltpu.make_async_copy(
                buf.at[:, here, pl.ds(keep, columns - 8), :],
                out.at[:, here, pl.ds(keep, columns - 8), :],
                sem.at[n, block // 8],
            )
            copy.start()
            copies.append(copy)
            tile[:, here] = buf[:, here, pl.ds(rest, 8), :]
    for copy in copies:
        copy.wait()


def last_columns(
    v_ref, s_tile, v_tile, halo, my_ref, v_in, s_in, v_out, s_out, v_buf, s_buf, sem
):
    comps, extent, columns, lanes = v_ref.shape
    odd = lax.rem(lax.axis_index("yz"), 2)
    u_rows = v_ref.reshape(comps * extent * columns, lanes)
    v_rows, s_rows = (r.reshape(comps * extent * 8, lanes) for r in (v_buf, s_buf))
    for side in range(2):

        @pl.when(odd == side)
        def _():
            first = columns - 8 if side else 0
            copies = []
            for c in range(comps):
                v_buf[c] = v_tile[c]
                s_buf[c] = s_tile[c]
            for block in range(0, extent, 8):

                def wide(c, j):
                    return pl.ds((c * extent + block) * columns + j, 8, stride=columns)

                def at(c, j):
                    return pl.ds((c * extent + block) * 8 + j - first, 8, stride=8)

                def store(c, j, section, velocity):
                    s_rows[at(c, j), :] = section
                    v_rows[at(c, j), :] = velocity

                fix_columns(
                    halo, 0, block, columns, my_ref, side == 1,
                    lambda j: u_rows[wide(1, j), :],
                    lambda c, j: s_rows[at(c, j), :],
                    lambda c, j: u_rows[wide(c, j), :],
                    store,
                )
                if block % 32 == 24 or block == extent - 8:
                    done = block + 8 - (block % 32 + 8)
                    here = pl.ds(done, block + 8 - done)
                    for n, (buf, out) in enumerate(((v_buf, v_out), (s_buf, s_out))):
                        copy = pltpu.make_async_copy(
                            buf.at[:, here], out.at[:, here, pl.ds(first, 8), :], sem.at[n, block // 32]
                        )
                        copy.start()
                        copies.append(copy)
            for copy in copies:
                copy.wait()


def local(velocity, section_sum, metric_x, metric_y, *, blocks_x, blocks_y):
    comps, extent, columns, lanes = velocity.shape
    table = Rows(extent * blocks_x, extent)
    f32 = jnp.float32
    shape = velocity.shape
    size = 4 * velocity.size
    plane = (comps, columns, lanes)
    strip = (comps * 3, extent, lanes)
    tile = (comps, extent, 8, lanes)
    pairs_y = swaps(blocks_y)
    pairs_x = swaps(blocks_x)
    dma = pltpu.SemaphoreType.DMA

    y_send_1 = pl.pallas_call(
        pack_y_first,
        out_shape=jax.ShapeDtypeStruct(strip, f32),
        in_specs=[HBM],
        out_specs=VMEM,
        scratch_shapes=[vmem(tile), dma],
        compiler_params=params(4),
        cost_estimate=cost(0, size // 4),
        name="pack_y_first",
    )(velocity)
    y_got_1 = lax.ppermute(y_send_1, "yz", pairs_y[0])
    y_send_2, x_send_1, x_send_2 = pl.pallas_call(
        pack_rest,
        out_shape=[
            jax.ShapeDtypeStruct(strip, f32),
            jax.ShapeDtypeStruct((comps, 2, columns, lanes), f32),
            jax.ShapeDtypeStruct((comps, 2, columns, lanes), f32),
        ],
        in_specs=[HBM],
        out_specs=[VMEM, VMEM, VMEM],
        scratch_shapes=[vmem(tile), dma((3,))],
        compiler_params=params(4),
        cost_estimate=cost(0, size // 3),
        name="pack_rest",
    )(velocity)
    x_got_1 = lax.ppermute(x_send_1, "gx", pairs_x[0])
    x_got_2 = lax.ppermute(x_send_2, "gx", pairs_x[1])
    y_got_2 = lax.ppermute(y_send_2, "yz", pairs_y[1])

    t = pl.pallas_call(
        y_part,
        out_shape=vmem(shape),
        in_specs=[VMEM, SMEM],
        out_specs=VMEM,
        compiler_params=params(4),
        cost_estimate=cost(9 * velocity.size, 2 * size),
        name="y_part",
    )(velocity, metric_y)

    g, end_1, end_2 = pl.pallas_call(
        functools.partial(sweep, table),
        out_shape=[vmem(shape), jax.ShapeDtypeStruct(plane, f32), jax.ShapeDtypeStruct(plane, f32)],
        in_specs=[VMEM] * 3,
        out_specs=[VMEM] * 3,
        compiler_params=params(4),
        cost_estimate=cost(8 * velocity.size, 2 * size),
        name="sweep",
    )(velocity, x_got_1, x_got_2)
    end_got_1 = lax.ppermute(end_1, "gx", pairs_x[0])
    end_got_2 = lax.ppermute(end_2, "gx", pairs_x[1])

    v_new, s_new, v_tile, s_tile = pl.pallas_call(
        functools.partial(finish, table),
        out_shape=[jax.ShapeDtypeStruct(shape, f32)] * 2 + [vmem(tile)] * 2,
        in_specs=[VMEM] * 7 + [SMEM, SMEM],
        out_specs=[HBM, HBM, VMEM, VMEM],
        scratch_shapes=[vmem(shape), vmem(shape), vmem(plane), dma((2, extent // 8))],
        compiler_params=params(12),
        cost_estimate=cost(12 * velocity.size, 4 * size),
        name="finish",
    )(velocity, section_sum, g, t, end_got_1, end_got_2, y_got_1, metric_x, metric_y)

    return pl.pallas_call(
        last_columns,
        out_shape=[jax.ShapeDtypeStruct(shape, f32)] * 2,
        in_specs=[VMEM] * 4 + [SMEM, HBM, HBM],
        out_specs=[HBM, HBM],
        scratch_shapes=[vmem(tile), vmem(tile), dma((2, extent // 32))],
        input_output_aliases={5: 0, 6: 1},
        compiler_params=params(4),
        cost_estimate=cost(0, size),
        name="last_columns",
    )(velocity, s_tile, v_tile, y_got_2, metric_y, v_new, s_new)


def solution(mesh):
    in_specs = (P(None, "gx", "yz", None), P(None, "gx", "yz", None), P("gx"), P("yz"))
    out_specs = (P(None, "gx", "yz", None), P(None, "gx", "yz", None))
    body = functools.partial(local, blocks_x=mesh.shape["gx"], blocks_y=mesh.shape["yz"])
    return jax.shard_map(body, mesh=mesh, in_specs=in_specs, out_specs=out_specs, check_vma=False)
```
